32 devices in a mesh: groups: 2 (over x), planes: 4 (over y, core), chan: 4 (over z).
Axes of the slice: x: 2, y: 2, z: 4, core: 2. Of those that a mesh axis runs over, the one named last changes fastest.
Arguments:
- field: float32 [2, 16, 128, 128, 128], P('groups', None, ('planes', 'chan')), parts along dimension 0, may hold values from -6 to 6
- cotangent: float32 [2, 16, 128, 128, 128], P('groups', None, ('planes', 'chan')), parts along dimension 0, may hold values from -6 to 6
- spec_weight: float32 [2, 16, 16, 64, 2048], P(None, None, None, 'planes', 'chan'), may hold values from -1.5 to 1.5
- point_weight: float32 [16, 16], replicated, may hold values from -1.5 to 1.5
- bias: float32 [16], replicated, may hold values from -3 to 3
Outputs:
- output: float32 [2, 16, 128, 128, 128], P('groups', None, ('planes', 'chan')), parts along dimension 0
- field_grad: float32 [2, 16, 128, 128, 128], P('groups', None, ('planes', 'chan')), parts along dimension 0
- weight_grad: float32 [4, 16, 16, 64, 2048], P('groups', None, None, 'planes', 'chan'), parts along dimension 0
The draws below stay inside these ranges and needn't reach their ends.
There are 2 independent parts, one for each index of `groups`. The reference program is written for one: setup_inputs(seed, part) draws one part's arguments, and reference() takes and returns one part's arrays. A program takes and returns all parts, laid end to end along the dimension named above; an argument that names none is the same for every part. Nothing has to cross between parts.
All inputs are finite; a program needn't handle non-finite values.
Results may differ from the reference program's by a relative error of at most 0.0001.
Values sent between devices are 32-bit elements; how exact they have to be, the bound alone decides.
A program may use at most 192 MiB of HBM per device.

```python
import jax
import jax.numpy as jnp
from jax import lax

CH = 16
GX = 128
GY = 128
GZ = 128
MODES = 32
BATCH = 1


def steps_of(rng, extent, cuts, low, high):
    def one(position, blocks):
        draws = jax.random.uniform(jax.random.fold_in(jax.random.fold_in(rng, 6), position), (blocks,), jnp.float32, low / len(cuts), high / len(cuts))
        return jnp.repeat(jnp.exp(draws), extent[position] // blocks).reshape((-1,) + (1,) * (len(extent) - position - 1))

    loudness = one(*cuts[0])
    for cut in cuts[1:]:
        loudness = loudness * one(*cut)
    return loudness


def normal_values(rng, dims, width, reach, shards=(), kind=jnp.bfloat16):
    gain = steps_of(rng, dims, shards, -0.22, 0.18) if shards else 1.0
    values = jax.random.normal(rng, dims, jnp.float32) * width * gain
    return jnp.minimum(jnp.maximum(values, -reach), reach).astype(kind)


def setup_inputs(seed: int = 0, part: int = 0) -> dict:
    keys = jax.random.split(jax.random.key(seed), 6)
    own_keys = jax.random.split(jax.random.fold_in(keys[5], part), 6)
    return {
        "field": normal_values(own_keys[0], (BATCH, CH, GX, GY, GZ), 1.0, 6.0, ((2, 16),), jnp.float32),
        "cotangent": normal_values(own_keys[1], (BATCH, CH, GX, GY, GZ), 1.0, 6.0, ((2, 16),), jnp.float32),
        "spec_weight": normal_values(keys[2], (2, CH, CH, 2 * MODES, 2 * MODES * MODES), CH ** -0.5, 1.5, ((3, 4), (4, 4)), jnp.float32),
        "point_weight": normal_values(keys[3], (CH, CH), CH ** -0.5, 1.5, (), jnp.float32),
        "bias": normal_values(keys[4], (CH,), 0.5, 3.0, (), jnp.float32),
    }


def retained_index(length):
    return jnp.concatenate([jnp.arange(MODES), jnp.arange(length - MODES, length)])

def layer(field_value, weight_value, point_weight, bias):
    first_modes = retained_index(GX)
    second_modes = retained_index(GY)
    transform = jnp.fft.rfftn(field_value, axes=(2, 3, 4))
    transform = jnp.take(transform, first_modes, axis=2)
    transform = jnp.take(transform, second_modes, axis=3)
    transform = transform[..., :MODES]
    spec_re = jnp.real(transform)
    spec_im = jnp.imag(transform)
    shaped = weight_value.reshape(2, CH, CH, 2 * MODES, 2 * MODES, MODES)
    weight_re = shaped[0]
    weight_im = shaped[1]

    def contract(operand, weights):
        return jnp.einsum('bifkm,iokfm->bofkm', operand, weights, precision=lax.Precision.HIGHEST)
    mixed_re = contract(spec_re, weight_re) - contract(spec_im, weight_im)
    mixed_im = contract(spec_re, weight_im) + contract(spec_im, weight_re)
    mixed_modes = lax.complex(mixed_re, mixed_im)
    filled = jnp.zeros((BATCH, CH, GX, GY, GZ // 2 + 1), dtype=mixed_modes.dtype)
    filled = filled.at[:, :, first_modes[:, None], second_modes[None, :], :MODES].set(mixed_modes)
    spectral = jnp.fft.irfftn(filled, s=(GX, GY, GZ), axes=(2, 3, 4))
    pointwise = jnp.einsum('bixyz,io->boxyz', field_value, point_weight, precision=lax.Precision.HIGHEST)
    preactivation = spectral + pointwise + bias[None, :, None, None, None]
    return jax.nn.gelu(preactivation, approximate=False)

def reference(field, cotangent, spec_weight, point_weight, bias):

    def closed(field_value, weight_value):
        return layer(field_value, weight_value, point_weight, bias)
    output, pullback = jax.vjp(closed, field, spec_weight)
    field_grad, weight_grad = pullback(cotangent)
    return (output, field_grad, weight_grad)
```

```python
import functools
import math

import jax
import jax.numpy as jnp
import numpy as np
from jax import lax
from jax.experimental import pallas as pl
from jax.experimental.pallas import tpu as pltpu
from jax.sharding import PartitionSpec as P

HIGH = lax.Precision.HIGH
F32 = jnp.float32
GRANT = 56 * 1024 * 1024


def dot(a, b):
    return jnp.dot(a, b, precision=HIGH, preferred_element_type=F32)


def angles(length, freqs):
    turns = np.outer(np.arange(length), freqs) % length
    return turns * (2.0 * math.pi / length)


def retained(length, modes):
    index = np.arange(2 * modes)
    return np.where(index < modes, index, length - 2 * modes + index)


class Tables:
    def __init__(self, gx, gy, gz, modes, width):
        ay = angles(gy, retained(gy, modes))
        self.y = np.concatenate([np.cos(ay).T, np.sin(ay).T], 0).astype(np.float32)
        self.y_inv = np.concatenate([np.cos(ay), np.sin(ay)], 1).astype(np.float32)
        az = angles(gz, np.arange(modes))
        cz, sz = np.cos(az), np.sin(az)
        z = np.zeros((width, 2, gz, 2, width, modes))
        z_inv = np.zeros((2, width, modes, width, 2, gz))
        for d in range(width):
            z[d, 0, :, 0, d] = cz
            z[d, 1, :, 0, d] = -sz
            z[d, 0, :, 1, d] = -sz
            z[d, 1, :, 1, d] = -cz
            z_inv[0, d, :, d, 0] = cz.T
            z_inv[1, d, :, d, 0] = -sz.T
            z_inv[0, d, :, d, 1] = -sz.T
            z_inv[1, d, :, d, 1] = -cz.T
        self.z = z.reshape(width * 2 * gz, 2 * width * modes).astype(np.float32)
        self.z_inv = z_inv.reshape(2 * width * modes, width * 2 * gz).astype(np.float32)
        ax = angles(gx, retained(gx, modes))
        self.x = np.concatenate([np.cos(ax).T, np.sin(ax).T], 0).astype(np.float32)
        self.x_inv = np.concatenate([np.cos(ax), np.sin(ax)], 1).astype(np.float32)


def analysis_rows(planes, y_table, z_table, channels, groups):
    second = dot(y_table, planes)
    rows = second.shape[0] // 2
    gz = planes.shape[1] // channels
    width = channels // groups
    stacked = []
    for c in range(groups):
        parts = []
        for d in range(width):
            lanes = slice((c * width + d) * gz, (c * width + d + 1) * gz)
            parts.append(second[:rows, lanes])
            parts.append(second[rows:, lanes])
        stacked.append(jnp.concatenate(parts, 1))
    return dot(jnp.concatenate(stacked, 0), z_table)


class Exchange:
    def __init__(self, plane_count, groups):
        self.groups = groups
        self.count = plane_count * groups
        self.plane = lax.axis_index("planes")
        self.chan = lax.axis_index("chan")
        self.me = self.plane * groups + self.chan

    def barrier(self):
        semaphore = pltpu.get_barrier_semaphore()

        def greet(offset, carry):
            other = lax.rem(self.me + offset, self.count)
            pl.semaphore_signal(
                semaphore,
                inc=1,
                device_id={"planes": other // self.groups, "chan": lax.rem(other, self.groups)},
                device_id_type=pl.DeviceIdType.MESH,
            )
            return carry

        lax.fori_loop(1, self.count, greet, 0)
        pl.semaphore_wait(semaphore, self.count - 1)

    def to_all(self, source, target, local_planes, x, send, recv):
        def one(offset, carry):
            other = lax.rem(self.me + offset, self.count)
            pltpu.make_async_remote_copy(
                src_ref=source.at[other * local_planes + x],
                dst_ref=target.at[self.me * local_planes + x],
                send_sem=send,
                recv_sem=recv,
                device_id={"planes": other // self.groups, "chan": lax.rem(other, self.groups)},
                device_id_type=pl.DeviceIdType.MESH,
            ).start()
            return carry

        lax.fori_loop(1, self.count, one, 0)

    def to_chan(self, source, target, send, recv):
        def one(offset, carry):
            other = lax.rem(self.chan + offset, self.groups)
            pltpu.make_async_remote_copy(
                src_ref=source(other),
                dst_ref=target(self.chan),
                send_sem=send,
                recv_sem=recv,
                device_id={"chan": other},
                device_id_type=pl.DeviceIdType.MESH,
            ).start()
            return carry

        lax.fori_loop(1, self.groups, one, 0)


def drain(ref, semaphore):
    pltpu.make_async_copy(ref, ref, semaphore).wait()


def send_plane(net, result, x, local_planes, kl, send, recv, sems):
    rows = net.count // net.groups * kl
    for c in range(net.groups):
        for p in range(net.count // net.groups):
            start = c * rows + p * kl
            send[(p * net.groups + c) * local_planes + x] = result[start : start + kl]
    mine = net.me * local_planes + x
    recv[mine] = send[mine]
    net.to_all(send, recv, local_planes, x, sems.at[0], sems.at[1])


def finish_analysis(net, table_ref, out_ref, send, recv, blocks, sems, local_planes):
    others = (net.count - 1) * local_planes
    drain(recv.at[pl.ds(0, others)], sems.at[1])
    table = table_ref[...]
    groups, kl, fl, lanes = blocks.shape
    half = lanes // 2
    rows = groups * fl
    for k in range(kl):
        both = dot(table, recv[:, k, :])
        cosine, sine = both[:rows], both[rows:]
        re = cosine[:, :half] + sine[:, half:]
        im = cosine[:, half:] - sine[:, :half]
        value = jnp.concatenate([re, im], 1)
        for c in range(groups):
            blocks[c, k] = value[c * fl : (c + 1) * fl]
        net.to_chan(
            lambda c: blocks.at[c, k], lambda c: out_ref.at[c, k], sems.at[2], sems.at[3]
        )
    own = pltpu.make_async_copy(blocks.at[net.chan], out_ref.at[net.chan], sems.at[4])
    own.start()
    own.wait()
    drain(send.at[pl.ds(0, others)], sems.at[0])
    drain(blocks.at[pl.ds(0, groups - 1)], sems.at[2])
    drain(out_ref.at[pl.ds(0, groups - 1)], sems.at[3])


def start_synthesis(net, in_ref, table_ref, blocks, send, recv, sems, plane_sems, local_planes):
    net.to_chan(
        lambda c: in_ref.at[c], lambda c: blocks.at[c], sems.at[0], sems.at[1]
    )
    own = pltpu.make_async_copy(in_ref.at[net.chan], blocks.at[net.chan], sems.at[2])
    own.start()
    own.wait()
    groups, kl, _, lanes = blocks.shape
    drain(blocks.at[pl.ds(0, groups - 1)], sems.at[1])
    table = table_ref[...]
    half = lanes // 2
    for k in range(kl):
        value = jnp.concatenate([blocks[c, k] for c in range(groups)], 0)
        turned = jnp.concatenate([-value[:, half:], value[:, :half]], 1)
        send[:, k, :] = dot(table, jnp.concatenate([value, turned], 0))
    mine = pl.ds(net.me * local_planes, local_planes)
    recv[mine] = send[mine]

    def plane(x, carry):
        net.to_all(send, recv, local_planes, x, sems.at[3], plane_sems.at[x])
        return carry

    lax.fori_loop(0, local_planes, plane, 0)


def finish_synthesis(net, in_ref, send, sems, local_planes):
    drain(in_ref.at[pl.ds(0, net.groups - 1)], sems.at[0])
    drain(send.at[pl.ds(0, (net.count - 1) * local_planes)], sems.at[3])


def synthesis_planes(net, recv, x, local_planes, y_inv, z_inv, channels):
    width = channels // net.groups
    gz = z_inv.shape[1] // (2 * width)
    kl = recv.shape[1]
    plane_count = net.count // net.groups
    rows = plane_count * kl
    stacked = [
        recv[(p * net.groups + c) * local_planes + x]
        for c in range(net.groups)
        for p in range(plane_count)
    ]
    depth = dot(jnp.concatenate(stacked, 0), z_inv)
    parts = []
    for c in range(net.groups):
        block = depth[c * rows : (c + 1) * rows]
        for d in range(width):
            base = 2 * d * gz
            parts.append(
                jnp.concatenate(
                    [block[:, base : base + gz], block[:, base + gz : base + 2 * gz]], 0
                )
            )
    return dot(y_inv, jnp.concatenate(parts, 1))


def first_kernel(
    plane_count, groups, field_ref, y_ref, z_ref, x_ref, out_ref, send, recv, blocks, sems
):
    net = Exchange(plane_count, groups)
    x, local_planes = pl.program_id(0), recv.shape[0] // net.count
    pl.when(x == 0)(net.barrier)
    channels = field_ref.shape[1]
    planes = jnp.concatenate([field_ref[0, i, 0] for i in range(channels)], 1)
    result = analysis_rows(planes, y_ref[...], z_ref[...], channels, groups)
    send_plane(net, result, x, local_planes, recv.shape[1], send, recv, sems)

    @pl.when(x == local_planes - 1)
    def _():
        finish_analysis(net, x_ref, out_ref, send, recv, blocks, sems, local_planes)


def middle_kernel(
    plane_count,
    groups,
    weight_ref,
    bias_ref,
    in_ref,
    field_ref,
    cot_ref,
    y_inv_ref,
    z_inv_ref,
    x_inv_ref,
    y_ref,
    z_ref,
    x_ref,
    out_ref,
    grad_ref,
    next_ref,
    spectral,
    pre_grad,
    back_blocks,
    back_send,
    back_recv,
    back_sems,
    plane_sems,
    send,
    recv,
    blocks,
    sems,
):
    net = Exchange(plane_count, groups)
    x, local_planes = pl.program_id(0), recv.shape[0] // net.count
    channels, gy, gz = field_ref.shape[1], field_ref.shape[3], field_ref.shape[4]

    @pl.when(x == 0)
    def _():
        net.barrier()
        start_synthesis(
            net,
            in_ref,
            x_inv_ref,
            back_blocks,
            back_send,
            back_recv,
            back_sems,
            plane_sems,
            local_planes,
        )

    drain(back_recv.at[pl.ds(0, net.count - 1)], plane_sems.at[x])
    spectral[...] = synthesis_planes(
        net, back_recv, x, local_planes, y_inv_ref[...], z_inv_ref[...], channels
    )
    step = 16

    def chunk(j, carry):
        rows = pl.ds(pl.multiple_of(j * step, step), step)
        inputs = [field_ref[0, i, 0, rows, :] for i in range(channels)]
        grads = []
        for o in range(channels):
            lanes = slice(o * gz, (o + 1) * gz)
            pre = spectral[rows, lanes] + bias_ref[o]
            for i in range(channels):
                pre = pre + inputs[i] * weight_ref[i, o]
            cdf = 0.5 * (1.0 + lax.erf(pre * (1.0 / math.sqrt(2.0))))
            out_ref[0, o, 0, rows, :] = pre * cdf
            slope = cdf + pre * jnp.exp(-0.5 * pre * pre) * (1.0 / math.sqrt(2.0 * math.pi))
            grad = cot_ref[0, o, 0, rows, :] * slope
            pre_grad[rows, lanes] = grad
            grads.append(grad)
        for i in range(channels):
            total = grads[0] * weight_ref[i, 0]
            for o in range(1, channels):
                total = total + grads[o] * weight_ref[i, o]
            grad_ref[0, i, 0, rows, :] = total
        return carry

    lax.fori_loop(0, gy // step, chunk, 0)
    result = analysis_rows(pre_grad[...], y_ref[...], z_ref[...], channels, groups)
    send_plane(net, result, x, local_planes, recv.shape[1], send, recv, sems)

    @pl.when(x == local_planes - 1)
    def _():
        finish_analysis(net, x_ref, next_ref, send, recv, blocks, sems, local_planes)
        finish_synthesis(net, in_ref, back_send, back_sems, local_planes)


def last_kernel(
    plane_count,
    groups,
    in_ref,
    grad_ref,
    y_inv_ref,
    z_inv_ref,
    x_inv_ref,
    out_ref,
    blocks,
    send,
    recv,
    sems,
    plane_sems,
):
    net = Exchange(plane_count, groups)
    x, local_planes = pl.program_id(0), recv.shape[0] // net.count
    channels, gz = grad_ref.shape[1], grad_ref.shape[4]

    @pl.when(x == 0)
    def _():
        net.barrier()
        start_synthesis(
            net, in_ref, x_inv_ref, blocks, send, recv, sems, plane_sems, local_planes
        )

    drain(recv.at[pl.ds(0, net.count - 1)], plane_sems.at[x])
    planes = synthesis_planes(
        net, recv, x, local_planes, y_inv_ref[...], z_inv_ref[...], channels
    )
    for i in range(channels):
        out_ref[0, i, 0] = grad_ref[0, i, 0] + planes[:, i * gz : (i + 1) * gz]

    @pl.when(x == local_planes - 1)
    def _():
        finish_synthesis(net, in_ref, send, sems, local_planes)


def mix_kernel(spec_ref, weight_ref, scale_ref, out_ref):
    channels = spec_ref.shape[1]
    scale = scale_ref[...]

    def one(o, carry):
        re = jnp.zeros(spec_ref.shape[2:], F32)
        im = re
        for i in range(channels):
            wr, wi = weight_ref[0, i, o], weight_ref[1, i, o]
            sr, si = spec_ref[0, i], spec_ref[1, i]
            re = re + (sr * wr - si * wi)
            im = im + (sr * wi + si * wr)
        out_ref[0, o] = re * scale
        out_ref[1, o] = im * scale
        return carry

    lax.fori_loop(0, weight_ref.shape[2], one, 0)


def back_kernel(grad_ref, weight_ref, scale_ref, out_ref):
    channels = grad_ref.shape[1]
    scale = scale_ref[...]

    def one(i, carry):
        re = jnp.zeros(grad_ref.shape[2:], F32)
        im = re
        for o in range(channels):
            wr, wi = weight_ref[0, i, o], weight_ref[1, i, o]
            gr, gi = grad_ref[0, o], grad_ref[1, o]
            re = re + (gr * wr + gi * wi)
            im = im + (gi * wr - gr * wi)
        out_ref[0, i] = re * scale
        out_ref[1, i] = im * scale
        return carry

    lax.fori_loop(0, weight_ref.shape[1], one, 0)


def outer_kernel(spec_ref, grad_ref, scale_ref, out_ref):
    channels = spec_ref.shape[1]
    scale = scale_ref[...]

    def one(i, carry):
        sr, si = spec_ref[0, i] * scale, spec_ref[1, i] * scale
        for o in range(channels):
            gr, gi = grad_ref[0, o], grad_ref[1, o]
            out_ref[0, i, o] = sr * gr + si * gi
            out_ref[1, i, o] = sr * gi - si * gr
        return carry

    lax.fori_loop(0, channels, one, 0)


def params(collective_id=None):
    if collective_id is None:
        return pltpu.CompilerParams(vmem_limit_bytes=GRANT)
    return pltpu.CompilerParams(
        vmem_limit_bytes=GRANT, collective_id=collective_id, has_side_effects=True
    )


def whole(array):
    return pl.BlockSpec(array.shape, lambda *_: (0,) * array.ndim)


def planes_spec(shape):
    return pl.BlockSpec((1, shape[1], 1, shape[3], shape[4]), lambda x: (0, 0, x, 0, 0))


def modes_spec(shape):
    tile = min(128, shape[-1])
    lead = len(shape) - 1
    return pl.BlockSpec(shape[:-1] + (tile,), lambda n: (0,) * lead + (n,))


def shape_of(dims):
    return jax.ShapeDtypeStruct(dims, F32)


def local(plane_count, groups, field, cotangent, spec_weight, point_weight, bias):
    _, channels, local_planes, gy, gz = field.shape
    gx = local_planes * plane_count * groups
    kl = spec_weight.shape[3]
    modes = kl * plane_count // 2
    fl = spec_weight.shape[4] // modes
    width = channels // groups
    lanes = 2 * width * modes
    tables = Tables(gx, gy, gz, modes, width)
    y, z, x = jnp.asarray(tables.y), jnp.asarray(tables.z), jnp.asarray(tables.x)
    y_inv, z_inv, x_inv = (
        jnp.asarray(tables.y_inv),
        jnp.asarray(tables.z_inv),
        jnp.asarray(tables.x_inv),
    )
    weighting = np.where(np.arange(fl * modes) % modes == 0, 1.0, 2.0) / float(gx * gy * gz)
    scale = jnp.asarray(weighting.astype(np.float32)[None, :])
    block_shape = (groups, kl, fl, lanes)
    mode_shape = (2, channels, kl, fl * modes)
    plane_rows = pltpu.VMEM((gx, kl, lanes), F32)
    mode_rows = pltpu.VMEM(block_shape, F32)
    semaphores = pltpu.SemaphoreType.DMA((5,))
    plane_semaphores = pltpu.SemaphoreType.DMA((local_planes,))
    anywhere = pl.BlockSpec(memory_space=pl.ANY)
    smem = pl.BlockSpec(memory_space=pltpu.SMEM)
    plane_block = planes_spec(field.shape)

    def to_modes(blocks):
        blocks = blocks.reshape(groups, kl, fl, 2, width, modes)
        return blocks.transpose(3, 0, 4, 1, 2, 5).reshape(mode_shape)

    def from_modes(mixed):
        blocks = mixed.reshape(2, groups, width, kl, fl, modes).transpose(1, 3, 4, 0, 2, 5)
        return blocks.reshape(block_shape)

    blocks = pl.pallas_call(
        functools.partial(first_kernel, plane_count, groups),
        grid=(local_planes,),
        in_specs=[plane_block, whole(y), whole(z), whole(x)],
        out_specs=anywhere,
        out_shape=shape_of(block_shape),
        scratch_shapes=[plane_rows, plane_rows, mode_rows, semaphores],
        compiler_params=params(1),
        name="first",
    )(field, y, z, x)
    spectrum = to_modes(blocks)
    mode_block = modes_spec(mode_shape)
    weight_block = modes_spec(spec_weight.shape)
    scale_block = modes_spec(scale.shape)
    mode_grid = (mode_shape[-1] // min(128, mode_shape[-1]),)
    mixed = pl.pallas_call(
        mix_kernel,
        grid=mode_grid,
        in_specs=[mode_block, weight_block, scale_block],
        out_specs=mode_block,
        out_shape=shape_of(mode_shape),
        compiler_params=params(),
        name="mix",
    )(spectrum, spec_weight, scale)
    output, local_grad, blocks = pl.pallas_call(
        functools.partial(middle_kernel, plane_count, groups),
        grid=(local_planes,),
        in_specs=[smem, smem, anywhere, plane_block, plane_block]
        + [whole(y_inv), whole(z_inv), whole(x_inv), whole(y), whole(z), whole(x)],
        out_specs=[plane_block, plane_block, anywhere],
        out_shape=[shape_of(field.shape), shape_of(field.shape), shape_of(block_shape)],
        scratch_shapes=[pltpu.VMEM((gy, channels * gz), F32)] * 2
        + [mode_rows, plane_rows, plane_rows, semaphores, plane_semaphores]
        + [plane_rows, plane_rows, mode_rows, semaphores],
        compiler_params=params(2),
        name="middle",
    )(
        point_weight,
        bias,
        from_modes(mixed),
        field,
        cotangent,
        y_inv,
        z_inv,
        x_inv,
        y,
        z,
        x,
    )
    grad_modes = to_modes(blocks)
    spectrum_grad = pl.pallas_call(
        back_kernel,
        grid=mode_grid,
        in_specs=[mode_block, weight_block, scale_block],
        out_specs=mode_block,
        out_shape=shape_of(mode_shape),
        compiler_params=params(),
        name="back",
    )(grad_modes, spec_weight, scale)
    weight_grad = pl.pallas_call(
        outer_kernel,
        grid=mode_grid,
        in_specs=[mode_block, mode_block, scale_block],
        out_specs=weight_block,
        out_shape=shape_of(spec_weight.shape),
        compiler_params=params(),
        name="weight_grad",
    )(spectrum, grad_modes, scale)
    field_grad = pl.pallas_call(
        functools.partial(last_kernel, plane_count, groups),
        grid=(local_planes,),
        in_specs=[anywhere, plane_block, whole(y_inv), whole(z_inv), whole(x_inv)],
        out_specs=plane_block,
        out_shape=shape_of(field.shape),
        scratch_shapes=[mode_rows, plane_rows, plane_rows, semaphores, plane_semaphores],
        compiler_params=params(3),
        name="last",
    )(from_modes(spectrum_grad), local_grad, y_inv, z_inv, x_inv)
    return (output, field_grad, weight_grad)


def solution(mesh):
    shard = P("groups", None, ("planes", "chan"), None, None)
    in_specs = (shard, shard, P(None, None, None, "planes", "chan"), P(), P())
    out_specs = (shard, shard, P("groups", None, None, "planes", "chan"))
    function = functools.partial(local, mesh.shape["planes"], mesh.shape["chan"])
    return jax.shard_map(
        function, mesh=mesh, in_specs=in_specs, out_specs=out_specs, check_vma=False
    )
```

```python
import functools
import math

import jax
import jax.numpy as jnp
import numpy as np
from jax import lax
from jax.experimental import pallas as pl
from jax.experimental.pallas import tpu as pltpu
from jax.sharding import PartitionSpec as P

HIGH = lax.Precision.HIGH
F32 = jnp.float32
GRANT = 56 * 1024 * 1024


def dot(a, b):
    return jnp.dot(a, b, precision=HIGH, preferred_element_type=F32)


def angles(length, freqs):
    turns = np.outer(np.arange(length), freqs) % length
    return turns * (2.0 * math.pi / length)


def retained(length, modes):
    index = np.arange(2 * modes)
    return np.where(index < modes, index, length - 2 * modes + index)


class Tables:
    def __init__(self, gx, gy, gz, modes, width, order):
        ay = angles(gy, retained(gy, modes))
        self.y = np.concatenate([np.cos(ay).T, np.sin(ay).T], 0).astype(np.float32)
        self.y_inv = np.concatenate([np.cos(ay), np.sin(ay)], 1).astype(np.float32)
        az = angles(gz, np.arange(modes))
        cz, sz = np.cos(az), np.sin(az)
        z = np.zeros((width, 2, gz, 2, width, modes))
        z_inv = np.zeros((2, width, modes, width, 2, gz))
        for d in range(width):
            z[d, 0, :, 0, d] = cz
            z[d, 1, :, 0, d] = -sz
            z[d, 0, :, 1, d] = -sz
            z[d, 1, :, 1, d] = -cz
            z_inv[0, d, :, d, 0] = cz.T
            z_inv[1, d, :, d, 0] = -sz.T
            z_inv[0, d, :, d, 1] = -sz.T
            z_inv[1, d, :, d, 1] = -cz.T
        self.z = z.reshape(width * 2 * gz, 2 * width * modes).astype(np.float32)
        self.z_inv = z_inv.reshape(2 * width * modes, width * 2 * gz).astype(np.float32)
        ax = angles(gx, retained(gx, modes)[order])
        self.x = np.concatenate([np.cos(ax).T, np.sin(ax).T], 0).astype(np.float32)
        self.x_inv = np.concatenate([np.cos(ax), np.sin(ax)], 1).astype(np.float32)


def analysis_rows(planes, y_table, z_table, channels, groups):
    second = dot(y_table, planes)
    rows = second.shape[0] // 2
    gz = planes.shape[1] // channels
    width = channels // groups
    stacked = []
    for c in range(groups):
        parts = []
        for d in range(width):
            lanes = slice((c * width + d) * gz, (c * width + d + 1) * gz)
            parts.append(second[:rows, lanes])
            parts.append(second[rows:, lanes])
        stacked.append(jnp.concatenate(parts, 1))
    return dot(jnp.concatenate(stacked, 0), z_table)


class Exchange:
    def __init__(self, plane_count, groups):
        self.groups = groups
        self.count = plane_count * groups
        self.plane = lax.axis_index("planes")
        self.chan = lax.axis_index("chan")
        self.me = self.plane * groups + self.chan

    def barrier(self):
        semaphore = pltpu.get_barrier_semaphore()

        def greet(offset, carry):
            other = lax.rem(self.me + offset, self.count)
            pl.semaphore_signal(
                semaphore,
                inc=1,
                device_id={"planes": other // self.groups, "chan": lax.rem(other, self.groups)},
                device_id_type=pl.DeviceIdType.MESH,
            )
            return carry

        lax.fori_loop(1, self.count, greet, 0)
        pl.semaphore_wait(semaphore, self.count - 1)

    def to_all(self, source, target, local_planes, x, send, recv):
        def one(offset, carry):
            other = lax.rem(self.me + offset, self.count)
            pltpu.make_async_remote_copy(
                src_ref=source.at[other * local_planes + x],
                dst_ref=target.at[self.me * local_planes + x],
                send_sem=send,
                recv_sem=recv,
                device_id={"planes": other // self.groups, "chan": lax.rem(other, self.groups)},
                device_id_type=pl.DeviceIdType.MESH,
            ).start()
            return carry

        lax.fori_loop(1, self.count, one, 0)

    def to_chan(self, source, target, send, recv):
        def one(offset, carry):
            other = lax.rem(self.chan + offset, self.groups)
            pltpu.make_async_remote_copy(
                src_ref=source(other),
                dst_ref=target(self.chan),
                send_sem=send,
                recv_sem=recv,
                device_id={"chan": other},
                device_id_type=pl.DeviceIdType.MESH,
            ).start()
            return carry

        lax.fori_loop(1, self.groups, one, 0)


def drain(ref, semaphore):
    pltpu.make_async_copy(ref, ref, semaphore).wait()


def send_plane(net, result, x, local_planes, kl, send, recv, sems):
    rows = net.count // net.groups * kl
    for c in range(net.groups):
        for p in range(net.count // net.groups):
            start = c * rows + p * kl
            send[(p * net.groups + c) * local_planes + x] = result[start : start + kl]
    mine = net.me * local_planes + x
    recv[mine] = send[mine]
    net.to_all(send, recv, local_planes, x, sems.at[0], sems.at[1])


def finish_analysis(net, table_ref, out_ref, send, recv, blocks, sems, local_planes):
    others = (net.count - 1) * local_planes
    drain(recv.at[pl.ds(0, others)], sems.at[1])
    table = table_ref[...]
    _, width, rows, kl, tile = blocks.shape
    tiles = rows // net.groups
    half = recv.shape[2] // 2
    modes = half // width
    per = tile // modes
    chunk = 8 if kl % 8 == 0 else kl

    def source(c, k):
        return blocks.at[:, :, pl.ds(c * tiles, tiles), pl.ds(k, chunk), :]

    def target(c, k):
        return out_ref.at[:, pl.ds(c * width, width), :, pl.ds(k, chunk), :]

    for k in range(kl):
        both = dot(table, recv[:, k, :])
        cosine, sine = both[: per * rows], both[per * rows :]
        re = cosine[:, :half] + sine[:, half:]
        im = cosine[:, half:] - sine[:, :half]
        for t, value in enumerate((re, im)):
            for d in range(width):
                lanes = slice(d * modes, (d + 1) * modes)
                blocks[t, d, :, k, :] = jnp.concatenate(
                    [value[j * rows : (j + 1) * rows, lanes] for j in range(per)], 1
                )
        if (k + 1) % chunk == 0:
            start = k + 1 - chunk
            net.to_chan(
                lambda c: source(c, start), lambda c: target(c, start), sems.at[2], sems.at[3]
            )
    own = pltpu.make_async_copy(
        blocks.at[:, :, pl.ds(net.chan * tiles, tiles), :, :],
        out_ref.at[:, pl.ds(net.chan * width, width), :, :, :],
        sems.at[4],
    )
    own.start()
    own.wait()
    drain(send.at[pl.ds(0, others)], sems.at[0])
    drain(blocks.at[:, :, pl.ds(0, rows - tiles), :, :], sems.at[2])
    drain(out_ref.at[:, pl.ds(0, (net.groups - 1) * width), :, :, :], sems.at[3])


def start_synthesis(net, in_ref, table_ref, blocks, send, recv, sems, plane_sems, local_planes):
    _, width, rows, kl, tile = blocks.shape
    tiles = rows // net.groups
    half = recv.shape[2] // 2
    modes = half // width
    per = tile // modes

    def source(c):
        return in_ref.at[:, pl.ds(c * width, width), :, :, :]

    def target(c):
        return blocks.at[:, :, pl.ds(c * tiles, tiles), :, :]

    net.to_chan(source, target, sems.at[0], sems.at[1])
    own = pltpu.make_async_copy(source(net.chan), target(net.chan), sems.at[2])
    own.start()
    own.wait()
    drain(blocks.at[:, :, pl.ds(0, rows - tiles), :, :], sems.at[1])
    table = table_ref[...]
    for k in range(kl):
        loaded = [[blocks[t, d, :, k, :] for d in range(width)] for t in range(2)]
        re, im = [
            jnp.concatenate(
                [
                    jnp.concatenate([part[:, j * modes : (j + 1) * modes] for part in parts], 1)
                    for j in range(per)
                ],
                0,
            )
            for parts in loaded
        ]
        value = jnp.concatenate([re, im], 1)
        turned = jnp.concatenate([-im, re], 1)
        send[:, k, :] = dot(table, jnp.concatenate([value, turned], 0))
    mine = pl.ds(net.me * local_planes, local_planes)
    recv[mine] = send[mine]

    def plane(x, carry):
        net.to_all(send, recv, local_planes, x, sems.at[3], plane_sems.at[x])
        return carry

    lax.fori_loop(0, local_planes, plane, 0)


def finish_synthesis(net, in_ref, send, sems, local_planes):
    width = in_ref.shape[1] // net.groups
    drain(in_ref.at[:, pl.ds(0, (net.groups - 1) * width), :, :, :], sems.at[0])
    drain(send.at[pl.ds(0, (net.count - 1) * local_planes)], sems.at[3])


def synthesis_planes(net, recv, x, local_planes, y_inv, z_inv, channels):
    width = channels // net.groups
    gz = z_inv.shape[1] // (2 * width)
    kl = recv.shape[1]
    plane_count = net.count // net.groups
    rows = plane_count * kl
    stacked = [
        recv[(p * net.groups + c) * local_planes + x]
        for c in range(net.groups)
        for p in range(plane_count)
    ]
    depth = dot(jnp.concatenate(stacked, 0), z_inv)
    parts = []
    for c in range(net.groups):
        block = depth[c * rows : (c + 1) * rows]
        for d in range(width):
            base = 2 * d * gz
            parts.append(
                jnp.concatenate(
                    [block[:, base : base + gz], block[:, base + gz : base + 2 * gz]], 0
                )
            )
    return dot(y_inv, jnp.concatenate(parts, 1))


def first_kernel(
    plane_count, groups, field_ref, y_ref, z_ref, x_ref, out_ref, send, recv, blocks, sems
):
    net = Exchange(plane_count, groups)
    x, local_planes = pl.program_id(0), recv.shape[0] // net.count
    pl.when(x == 0)(net.barrier)
    channels = field_ref.shape[1]
    planes = jnp.concatenate([field_ref[0, i, 0] for i in range(channels)], 1)
    result = analysis_rows(planes, y_ref[...], z_ref[...], channels, groups)
    send_plane(net, result, x, local_planes, recv.shape[1], send, recv, sems)

    @pl.when(x == local_planes - 1)
    def _():
        finish_analysis(net, x_ref, out_ref, send, recv, blocks, sems, local_planes)


def middle_kernel(
    plane_count,
    groups,
    weight_ref,
    bias_ref,
    in_ref,
    field_ref,
    cot_ref,
    y_inv_ref,
    z_inv_ref,
    x_inv_ref,
    y_ref,
    z_ref,
    x_ref,
    out_ref,
    grad_ref,
    next_ref,
    spectral,
    pre_grad,
    back_blocks,
    back_send,
    back_recv,
    back_sems,
    plane_sems,
    send,
    recv,
    blocks,
    sems,
):
    net = Exchange(plane_count, groups)
    x, local_planes = pl.program_id(0), recv.shape[0] // net.count
    channels, gy, gz = field_ref.shape[1], field_ref.shape[3], field_ref.shape[4]

    @pl.when(x == 0)
    def _():
        net.barrier()
        start_synthesis(
            net,
            in_ref,
            x_inv_ref,
            back_blocks,
            back_send,
            back_recv,
            back_sems,
            plane_sems,
            local_planes,
        )

    drain(back_recv.at[pl.ds(0, net.count - 1)], plane_sems.at[x])
    spectral[...] = synthesis_planes(
        net, back_recv, x, local_planes, y_inv_ref[...], z_inv_ref[...], channels
    )
    step = 16

    def chunk(j, carry):
        rows = pl.ds(pl.multiple_of(j * step, step), step)
        inputs = [field_ref[0, i, 0, rows, :] for i in range(channels)]
        grads = []
        for o in range(channels):
            lanes = slice(o * gz, (o + 1) * gz)
            pre = spectral[rows, lanes] + bias_ref[o]
            for i in range(channels):
                pre = pre + inputs[i] * weight_ref[i, o]
            cdf = 0.5 * (1.0 + lax.erf(pre * (1.0 / math.sqrt(2.0))))
            out_ref[0, o, 0, rows, :] = pre * cdf
            slope = cdf + pre * jnp.exp(-0.5 * pre * pre) * (1.0 / math.sqrt(2.0 * math.pi))
            grad = cot_ref[0, o, 0, rows, :] * slope
            pre_grad[rows, lanes] = grad
            grads.append(grad)
        for i in range(channels):
            total = grads[0] * weight_ref[i, 0]
            for o in range(1, channels):
                total = total + grads[o] * weight_ref[i, o]
            grad_ref[0, i, 0, rows, :] = total
        return carry

    lax.fori_loop(0, gy // step, chunk, 0)
    result = analysis_rows(pre_grad[...], y_ref[...], z_ref[...], channels, groups)
    send_plane(net, result, x, local_planes, recv.shape[1], send, recv, sems)

    @pl.when(x == local_planes - 1)
    def _():
        finish_analysis(net, x_ref, next_ref, send, recv, blocks, sems, local_planes)
        finish_synthesis(net, in_ref, back_send, back_sems, local_planes)


def last_kernel(
    plane_count,
    groups,
    in_ref,
    grad_ref,
    y_inv_ref,
    z_inv_ref,
    x_inv_ref,
    out_ref,
    blocks,
    send,
    recv,
    sems,
    plane_sems,
):
    net = Exchange(plane_count, groups)
    x, local_planes = pl.program_id(0), recv.shape[0] // net.count
    channels, gz = grad_ref.shape[1], grad_ref.shape[4]

    @pl.when(x == 0)
    def _():
        net.barrier()
        start_synthesis(
            net, in_ref, x_inv_ref, blocks, send, recv, sems, plane_sems, local_planes
        )

    drain(recv.at[pl.ds(0, net.count - 1)], plane_sems.at[x])
    planes = synthesis_planes(
        net, recv, x, local_planes, y_inv_ref[...], z_inv_ref[...], channels
    )
    for i in range(channels):
        out_ref[0, i, 0] = grad_ref[0, i, 0] + planes[:, i * gz : (i + 1) * gz]

    @pl.when(x == local_planes - 1)
    def _():
        finish_synthesis(net, in_ref, send, sems, local_planes)


def mix_kernel(spec_ref, weight_ref, scale_ref, out_ref):
    channels = spec_ref.shape[1]
    scale = scale_ref[...]
    spec = [(spec_ref[0, i, 0], spec_ref[1, i, 0]) for i in range(channels)]

    def one(o, carry):
        re = jnp.zeros(spec_ref.shape[3:], F32)
        im = re
        for i in range(channels):
            wr, wi = weight_ref[0, i, o], weight_ref[1, i, o]
            sr, si = spec[i]
            re = re + (sr * wr - si * wi)
            im = im + (sr * wi + si * wr)
        out_ref[0, o, 0] = re * scale
        out_ref[1, o, 0] = im * scale
        return carry

    lax.fori_loop(0, weight_ref.shape[2], one, 0)


def back_kernel(
    spec_ref, grad_ref, weight_ref, scale_ref, result_ref, out_ref, outer_ref, passed_ref
):
    channels = grad_ref.shape[1]
    scale = scale_ref[...]
    grads = [(grad_ref[0, o, 0] * scale, grad_ref[1, o, 0] * scale) for o in range(channels)]
    passed_ref[...] = result_ref[...]

    def one(i, carry):
        sr, si = spec_ref[0, i, 0], spec_ref[1, i, 0]
        re = jnp.zeros(grad_ref.shape[3:], F32)
        im = re
        for o in range(channels):
            wr, wi = weight_ref[0, i, o], weight_ref[1, i, o]
            gr, gi = grads[o]
            re = re + (gr * wr + gi * wi)
            im = im + (gi * wr - gr * wi)
            outer_ref[0, i, o] = sr * gr + si * gi
            outer_ref[1, i, o] = sr * gi - si * gr
        out_ref[0, i, 0] = re
        out_ref[1, i, 0] = im
        return carry

    lax.fori_loop(0, weight_ref.shape[1], one, 0)


def params(collective_id=None):
    if collective_id is None:
        return pltpu.CompilerParams(vmem_limit_bytes=GRANT)
    return pltpu.CompilerParams(
        vmem_limit_bytes=GRANT, collective_id=collective_id, has_side_effects=True
    )


def whole(array):
    return pl.BlockSpec(array.shape, lambda *_: (0,) * array.ndim)


def planes_spec(shape):
    return pl.BlockSpec((1, shape[1], 1, shape[3], shape[4]), lambda x: (0, 0, x, 0, 0))


def shape_of(dims):
    return jax.ShapeDtypeStruct(dims, F32)


def local(plane_count, groups, field, cotangent, spec_weight, point_weight, bias):
    _, channels, local_planes, gy, gz = field.shape
    gx = local_planes * plane_count * groups
    kl = spec_weight.shape[3]
    modes = kl * plane_count // 2
    fl = spec_weight.shape[4] // modes
    width = channels // groups
    lanes = 2 * width * modes
    tile = min(128, fl * modes)
    per, tiles = tile // modes, fl * modes // tile
    order = np.arange(2 * modes).reshape(groups, tiles, per).transpose(2, 0, 1).reshape(-1)
    tables = Tables(gx, gy, gz, modes, width, order)
    y, z, x = jnp.asarray(tables.y), jnp.asarray(tables.z), jnp.asarray(tables.x)
    y_inv, z_inv, x_inv = (
        jnp.asarray(tables.y_inv),
        jnp.asarray(tables.z_inv),
        jnp.asarray(tables.x_inv),
    )
    weighting = np.where(np.arange(tile) % modes == 0, 1.0, 2.0) / float(gx * gy * gz)
    scale = jnp.asarray(weighting.astype(np.float32)[None, :])
    mode_shape = (2, channels, tiles, kl, tile)
    plane_rows = pltpu.VMEM((gx, kl, lanes), F32)
    mode_rows = pltpu.VMEM((2, width, groups * tiles, kl, tile), F32)
    semaphores = pltpu.SemaphoreType.DMA((5,))
    plane_semaphores = pltpu.SemaphoreType.DMA((local_planes,))
    anywhere = pl.BlockSpec(memory_space=pl.ANY)
    smem = pl.BlockSpec(memory_space=pltpu.SMEM)
    plane_block = planes_spec(field.shape)

    spectrum = pl.pallas_call(
        functools.partial(first_kernel, plane_count, groups),
        grid=(local_planes,),
        in_specs=[plane_block, whole(y), whole(z), whole(x)],
        out_specs=anywhere,
        out_shape=shape_of(mode_shape),
        scratch_shapes=[plane_rows, plane_rows, mode_rows, semaphores],
        compiler_params=params(1),
        name="first",
    )(field, y, z, x)
    rows = 8 if kl % 8 == 0 else kl
    mode_grid = (tiles, kl // rows)
    mode_block = pl.BlockSpec((2, channels, 1, rows, tile), lambda n, k: (0, 0, n, k, 0))
    weight_block = pl.BlockSpec((2, channels, channels, rows, tile), lambda n, k: (0, 0, 0, k, n))
    scale_block = whole(scale)
    mixed = pl.pallas_call(
        mix_kernel,
        grid=mode_grid,
        in_specs=[mode_block, weight_block, scale_block],
        out_specs=mode_block,
        out_shape=shape_of(mode_shape),
        compiler_params=params(),
        name="mix",
    )(spectrum, spec_weight, scale)
    output, local_grad, grad_modes = pl.pallas_call(
        functools.partial(middle_kernel, plane_count, groups),
        grid=(local_planes,),
        in_specs=[smem, smem, anywhere, plane_block, plane_block]
        + [whole(y_inv), whole(z_inv), whole(x_inv), whole(y), whole(z), whole(x)],
        out_specs=[plane_block, plane_block, anywhere],
        out_shape=[shape_of(field.shape), shape_of(field.shape), shape_of(mode_shape)],
        scratch_shapes=[pltpu.VMEM((gy, channels * gz), F32)] * 2
        + [mode_rows, plane_rows, plane_rows, semaphores, plane_semaphores]
        + [plane_rows, plane_rows, mode_rows, semaphores],
        compiler_params=params(2),
        name="middle",
    )(
        point_weight,
        bias,
        mixed,
        field,
        cotangent,
        y_inv,
        z_inv,
        x_inv,
        y,
        z,
        x,
    )
    steps = tiles * (kl // rows)
    flat = output.reshape(-1, gz)
    flat_block = pl.BlockSpec(
        (flat.shape[0] // steps, gz), lambda n, k: (n * (kl // rows) + k, 0)
    )
    spectrum_grad, weight_grad, flat = pl.pallas_call(
        back_kernel,
        grid=mode_grid,
        in_specs=[mode_block, mode_block, weight_block, scale_block, flat_block],
        out_specs=[mode_block, weight_block, flat_block],
        out_shape=[shape_of(mode_shape), shape_of(spec_weight.shape), shape_of(flat.shape)],
        compiler_params=params(),
        name="back",
    )(spectrum, grad_modes, spec_weight, scale, flat)
    output = flat.reshape(output.shape)
    field_grad = pl.pallas_call(
        functools.partial(last_kernel, plane_count, groups),
        grid=(local_planes,),
        in_specs=[anywhere, plane_block, whole(y_inv), whole(z_inv), whole(x_inv)],
        out_specs=plane_block,
        out_shape=shape_of(field.shape),
        scratch_shapes=[mode_rows, plane_rows, plane_rows, semaphores, plane_semaphores],
        compiler_params=params(3),
        name="last",
    )(spectrum_grad, local_grad, y_inv, z_inv, x_inv)
    return (output, field_grad, weight_grad)


def solution(mesh):
    shard = P("groups", None, ("planes", "chan"), None, None)
    in_specs = (shard, shard, P(None, None, None, "planes", "chan"), P(), P())
    out_specs = (shard, shard, P("groups", None, None, "planes", "chan"))
    function = functools.partial(local, mesh.shape["planes"], mesh.shape["chan"])
    return jax.shard_map(
        function, mesh=mesh, in_specs=in_specs, out_specs=out_specs, check_vma=False
    )
```

```python
import functools
import math

import jax
import jax.numpy as jnp
import numpy as np
from jax import lax
from jax.experimental import pallas as pl
from jax.experimental.pallas import tpu as pltpu
from jax.sharding import PartitionSpec as P

HIGH = lax.Precision.HIGH
F32 = jnp.float32
GRANT = 56 * 1024 * 1024


def dot(a, b):
    return jnp.dot(a, b, precision=HIGH, preferred_element_type=F32)


def angles(length, freqs):
    turns = np.outer(np.arange(length), freqs) % length
    return turns * (2.0 * math.pi / length)


def retained(length, modes):
    index = np.arange(2 * modes)
    return np.where(index < modes, index, length - 2 * modes + index)


class Tables:
    def __init__(self, gx, gy, gz, modes, width, order):
        ay = angles(gy, retained(gy, modes))
        self.y = np.concatenate([np.cos(ay).T, np.sin(ay).T], 0).astype(np.float32)
        self.y_inv = np.concatenate([np.cos(ay), np.sin(ay)], 1).astype(np.float32)
        az = angles(gz, np.arange(modes))
        cz, sz = np.cos(az), np.sin(az)
        z = np.zeros((width, 2, gz, 2, width, modes))
        z_inv = np.zeros((2, width, modes, width, 2, gz))
        for d in range(width):
            z[d, 0, :, 0, d] = cz
            z[d, 1, :, 0, d] = -sz
            z[d, 0, :, 1, d] = -sz
            z[d, 1, :, 1, d] = -cz
            z_inv[0, d, :, d, 0] = cz.T
            z_inv[1, d, :, d, 0] = -sz.T
            z_inv[0, d, :, d, 1] = -sz.T
            z_inv[1, d, :, d, 1] = -cz.T
        self.z = z.reshape(width * 2 * gz, 2 * width * modes).astype(np.float32)
        self.z_inv = z_inv.reshape(2 * width * modes, width * 2 * gz).astype(np.float32)
        ax = angles(gx, retained(gx, modes)[order])
        self.x = np.concatenate([np.cos(ax).T, np.sin(ax).T], 0).astype(np.float32)
        self.x_inv = np.concatenate([np.cos(ax), np.sin(ax)], 1).astype(np.float32)


def analysis_rows(planes, y_table, z_table, channels, groups):
    second = dot(y_table, planes)
    rows = second.shape[0] // 2
    gz = planes.shape[1] // channels
    width = channels // groups
    stacked = []
    for c in range(groups):
        parts = []
        for d in range(width):
            lanes = slice((c * width + d) * gz, (c * width + d + 1) * gz)
            parts.append(second[:rows, lanes])
            parts.append(second[rows:, lanes])
        stacked.append(jnp.concatenate(parts, 1))
    return dot(jnp.concatenate(stacked, 0), z_table)


class Exchange:
    def __init__(self, plane_count, groups):
        self.groups = groups
        self.count = plane_count * groups
        self.plane = lax.axis_index("planes")
        self.chan = lax.axis_index("chan")
        self.me = self.plane * groups + self.chan

    def barrier(self):
        semaphore = pltpu.get_barrier_semaphore()

        def greet(offset, carry):
            other = lax.rem(self.me + offset, self.count)
            pl.semaphore_signal(
                semaphore,
                inc=1,
                device_id={"planes": other // self.groups, "chan": lax.rem(other, self.groups)},
                device_id_type=pl.DeviceIdType.MESH,
            )
            return carry

        lax.fori_loop(1, self.count, greet, 0)
        pl.semaphore_wait(semaphore, self.count - 1)

    def to_all(self, source, target, local_planes, x, ky, send, recv):
        def one(offset, carry):
            other = lax.rem(self.me + offset, self.count)
            pltpu.make_async_remote_copy(
                src_ref=source.at[other * local_planes + x, ky, :],
                dst_ref=target.at[self.me * local_planes + x, ky, :],
                send_sem=send,
                recv_sem=recv,
                device_id={"planes": other // self.groups, "chan": lax.rem(other, self.groups)},
                device_id_type=pl.DeviceIdType.MESH,
            ).start()
            return carry

        lax.fori_loop(1, self.count, one, 0)

    def to_chan(self, source, target, send, recv):
        def one(offset, carry):
            other = lax.rem(self.chan + offset, self.groups)
            pltpu.make_async_remote_copy(
                src_ref=source(other),
                dst_ref=target(self.chan),
                send_sem=send,
                recv_sem=recv,
                device_id={"chan": other},
                device_id_type=pl.DeviceIdType.MESH,
            ).start()
            return carry

        lax.fori_loop(1, self.groups, one, 0)


def pieces(kl):
    size = 8 if kl % 8 == 0 else kl
    return [pl.ds(start, size) for start in range(0, kl, size)]


def drain(ref, semaphore):
    pltpu.make_async_copy(ref, ref, semaphore).wait()


def send_plane(net, result, x, local_planes, kl, send, recv, sems, hold):
    rows = net.count // net.groups * kl
    for c in range(net.groups):
        for p in range(net.count // net.groups):
            start = c * rows + p * kl
            send[(p * net.groups + c) * local_planes + x] = result[start : start + kl]
    mine = net.me * local_planes + x
    recv[mine] = send[mine]
    cuts = pieces(kl) if hold else [pl.ds(0, kl)]
    for h, ky in enumerate(cuts[:1]):
        net.to_all(send, recv, local_planes, x, ky, sems.at[0], sems.at[5 + h])
    if len(cuts) == 1:
        return

    @pl.when(x == local_planes - 1)
    def _():
        for h, ky in list(enumerate(cuts))[1:]:

            def plane(row, carry):
                net.to_all(send, recv, local_planes, row, ky, sems.at[0], sems.at[5 + h])
                return carry

            lax.fori_loop(0, local_planes, plane, 0)


def finish_analysis(net, table_ref, out_ref, send, recv, blocks, sems, local_planes, hold):
    others = (net.count - 1) * local_planes
    table = table_ref[...]
    _, width, rows, kl, tile = blocks.shape
    tiles = rows // net.groups
    half = recv.shape[2] // 2
    modes = half // width
    per = tile // modes
    chunk = 8 if kl % 8 == 0 else kl
    piece = chunk if hold else kl

    def source(c, k):
        return blocks.at[:, :, pl.ds(c * tiles, tiles), pl.ds(k, chunk), :]

    def target(c, k):
        return out_ref.at[:, pl.ds(c * width, width), :, pl.ds(k, chunk), :]

    for k in range(kl):
        if k % piece == 0:
            drain(recv.at[pl.ds(0, others), pl.ds(k, piece), :], sems.at[5 + k // piece])
        both = dot(table, recv[:, k, :])
        cosine, sine = both[: per * rows], both[per * rows :]
        re = cosine[:, :half] + sine[:, half:]
        im = cosine[:, half:] - sine[:, :half]
        for t, value in enumerate((re, im)):
            for d in range(width):
                lanes = slice(d * modes, (d + 1) * modes)
                blocks[t, d, :, k, :] = jnp.concatenate(
                    [value[j * rows : (j + 1) * rows, lanes] for j in range(per)], 1
                )
        if (k + 1) % chunk == 0:
            start = k + 1 - chunk
            net.to_chan(
                lambda c: source(c, start), lambda c: target(c, start), sems.at[2], sems.at[3]
            )
    own = pltpu.make_async_copy(
        blocks.at[:, :, pl.ds(net.chan * tiles, tiles), :, :],
        out_ref.at[:, pl.ds(net.chan * width, width), :, :, :],
        sems.at[4],
    )
    own.start()
    own.wait()
    drain(send.at[pl.ds(0, others)], sems.at[0])
    drain(blocks.at[:, :, pl.ds(0, rows - tiles), :, :], sems.at[2])
    drain(out_ref.at[:, pl.ds(0, (net.groups - 1) * width), :, :, :], sems.at[3])


def start_synthesis(
    net, in_ref, table_ref, blocks, send, recv, sems, plane_sems, local_planes, early
):
    _, width, rows, kl, tile = blocks.shape
    tiles = rows // net.groups
    half = recv.shape[2] // 2
    modes = half // width
    per = tile // modes

    def source(c, ky):
        return in_ref.at[:, pl.ds(c * width, width), :, ky, :]

    def target(c, ky):
        return blocks.at[:, :, pl.ds(c * tiles, tiles), ky, :]

    cuts = pieces(kl)
    size = kl // len(cuts)
    for h, ky in enumerate(cuts):
        net.to_chan(
            lambda c: source(c, ky), lambda c: target(c, ky), sems.at[0], sems.at[5 + h]
        )
    every = pl.ds(0, kl)
    own = pltpu.make_async_copy(source(net.chan, every), target(net.chan, every), sems.at[2])
    own.start()
    own.wait()
    table = table_ref[...]

    def send_planes(ky):
        def plane(x, carry):
            net.to_all(send, recv, local_planes, x, ky, sems.at[3], plane_sems.at[x])
            return carry

        lax.fori_loop(0, local_planes, plane, 0)

    for k in range(kl):
        if k % size == 0:
            h = k // size
            drain(blocks.at[:, :, pl.ds(0, rows - tiles), cuts[h], :], sems.at[5 + h])
        loaded = [[blocks[t, d, :, k, :] for d in range(width)] for t in range(2)]
        re, im = [
            jnp.concatenate(
                [
                    jnp.concatenate([part[:, j * modes : (j + 1) * modes] for part in parts], 1)
                    for j in range(per)
                ],
                0,
            )
            for parts in loaded
        ]
        value = jnp.concatenate([re, im], 1)
        turned = jnp.concatenate([-im, re], 1)
        send[:, k, :] = dot(table, jnp.concatenate([value, turned], 0))
        if early and (k + 1) % size == 0:
            send_planes(cuts[k // size])
    if not early:
        send_planes(every)
    mine = pl.ds(net.me * local_planes, local_planes)
    recv[mine] = send[mine]


def finish_synthesis(net, in_ref, send, sems, local_planes):
    width = in_ref.shape[1] // net.groups
    drain(in_ref.at[:, pl.ds(0, (net.groups - 1) * width), :, :, :], sems.at[0])
    drain(send.at[pl.ds(0, (net.count - 1) * local_planes)], sems.at[3])


def synthesis_planes(net, recv, x, local_planes, y_inv, z_inv, channels):
    width = channels // net.groups
    gz = z_inv.shape[1] // (2 * width)
    kl = recv.shape[1]
    plane_count = net.count // net.groups
    rows = plane_count * kl
    stacked = [
        recv[(p * net.groups + c) * local_planes + x]
        for c in range(net.groups)
        for p in range(plane_count)
    ]
    depth = dot(jnp.concatenate(stacked, 0), z_inv)
    parts = []
    for c in range(net.groups):
        block = depth[c * rows : (c + 1) * rows]
        for d in range(width):
            base = 2 * d * gz
            parts.append(
                jnp.concatenate(
                    [block[:, base : base + gz], block[:, base + gz : base + 2 * gz]], 0
                )
            )
    return dot(y_inv, jnp.concatenate(parts, 1))


def first_kernel(
    plane_count, groups, field_ref, y_ref, z_ref, x_ref, out_ref, send, recv, blocks, sems
):
    net = Exchange(plane_count, groups)
    x, local_planes = pl.program_id(0), recv.shape[0] // net.count
    pl.when(x == 0)(net.barrier)
    channels = field_ref.shape[1]
    planes = jnp.concatenate([field_ref[0, i, 0] for i in range(channels)], 1)
    result = analysis_rows(planes, y_ref[...], z_ref[...], channels, groups)
    send_plane(net, result, x, local_planes, recv.shape[1], send, recv, sems, True)

    @pl.when(x == local_planes - 1)
    def _():
        finish_analysis(net, x_ref, out_ref, send, recv, blocks, sems, local_planes, True)


def middle_kernel(
    plane_count,
    groups,
    weight_ref,
    bias_ref,
    in_ref,
    field_ref,
    cot_ref,
    y_inv_ref,
    z_inv_ref,
    x_inv_ref,
    y_ref,
    z_ref,
    x_ref,
    out_ref,
    grad_ref,
    next_ref,
    spectral,
    pre_grad,
    back_blocks,
    back_send,
    back_recv,
    back_sems,
    plane_sems,
    send,
    recv,
    blocks,
    sems,
):
    net = Exchange(plane_count, groups)
    x, local_planes = pl.program_id(0), recv.shape[0] // net.count
    channels, gy, gz = field_ref.shape[1], field_ref.shape[3], field_ref.shape[4]

    @pl.when(x == 0)
    def _():
        net.barrier()
        start_synthesis(
            net,
            in_ref,
            x_inv_ref,
            back_blocks,
            back_send,
            back_recv,
            back_sems,
            plane_sems,
            local_planes,
            False,
        )

    drain(back_recv.at[pl.ds(0, net.count - 1)], plane_sems.at[x])
    spectral[...] = synthesis_planes(
        net, back_recv, x, local_planes, y_inv_ref[...], z_inv_ref[...], channels
    )
    step = 16

    def chunk(j, carry):
        rows = pl.ds(pl.multiple_of(j * step, step), step)
        inputs = [field_ref[0, i, 0, rows, :] for i in range(channels)]
        grads = []
        for o in range(channels):
            lanes = slice(o * gz, (o + 1) * gz)
            pre = spectral[rows, lanes] + bias_ref[o]
            for i in range(channels):
                pre = pre + inputs[i] * weight_ref[i, o]
            cdf = 0.5 * (1.0 + lax.erf(pre * (1.0 / math.sqrt(2.0))))
            out_ref[0, o, 0, rows, :] = pre * cdf
            slope = cdf + pre * jnp.exp(-0.5 * pre * pre) * (1.0 / math.sqrt(2.0 * math.pi))
            grad = cot_ref[0, o, 0, rows, :] * slope
            pre_grad[rows, lanes] = grad
            grads.append(grad)
        for i in range(channels):
            total = grads[0] * weight_ref[i, 0]
            for o in range(1, channels):
                total = total + grads[o] * weight_ref[i, o]
            grad_ref[0, i, 0, rows, :] = total
        return carry

    lax.fori_loop(0, gy // step, chunk, 0)
    result = analysis_rows(pre_grad[...], y_ref[...], z_ref[...], channels, groups)
    send_plane(net, result, x, local_planes, recv.shape[1], send, recv, sems, False)

    @pl.when(x == local_planes - 1)
    def _():
        finish_analysis(net, x_ref, next_ref, send, recv, blocks, sems, local_planes, False)
        finish_synthesis(net, in_ref, back_send, back_sems, local_planes)


def last_kernel(
    plane_count,
    groups,
    in_ref,
    grad_ref,
    y_inv_ref,
    z_inv_ref,
    x_inv_ref,
    out_ref,
    blocks,
    send,
    recv,
    sems,
    plane_sems,
):
    net = Exchange(plane_count, groups)
    x, local_planes = pl.program_id(0), recv.shape[0] // net.count
    channels, gz = grad_ref.shape[1], grad_ref.shape[4]

    @pl.when(x == 0)
    def _():
        net.barrier()
        start_synthesis(
            net, in_ref, x_inv_ref, blocks, send, recv, sems, plane_sems, local_planes, True
        )

    drain(recv.at[pl.ds(0, net.count - 1)], plane_sems.at[x])
    planes = synthesis_planes(
        net, recv, x, local_planes, y_inv_ref[...], z_inv_ref[...], channels
    )
    for i in range(channels):
        out_ref[0, i, 0] = grad_ref[0, i, 0] + planes[:, i * gz : (i + 1) * gz]

    @pl.when(x == local_planes - 1)
    def _():
        finish_synthesis(net, in_ref, send, sems, local_planes)


def mix_kernel(spec_ref, weight_ref, scale_ref, out_ref):
    channels = spec_ref.shape[1]
    scale = scale_ref[...]
    spec = [(spec_ref[0, i, 0], spec_ref[1, i, 0]) for i in range(channels)]

    def one(o, carry):
        re = jnp.zeros(spec_ref.shape[3:], F32)
        im = re
        for i in range(channels):
            wr, wi = weight_ref[0, i, o], weight_ref[1, i, o]
            sr, si = spec[i]
            re = re + (sr * wr - si * wi)
            im = im + (sr * wi + si * wr)
        out_ref[0, o, 0] = re * scale
        out_ref[1, o, 0] = im * scale
        return carry

    lax.fori_loop(0, weight_ref.shape[2], one, 0)


def back_kernel(
    spec_ref, grad_ref, weight_ref, scale_ref, result_ref, out_ref, outer_ref, passed_ref
):
    channels = grad_ref.shape[1]
    scale = scale_ref[...]
    grads = [(grad_ref[0, o, 0] * scale, grad_ref[1, o, 0] * scale) for o in range(channels)]
    passed_ref[...] = result_ref[...]

    def one(i, carry):
        sr, si = spec_ref[0, i, 0], spec_ref[1, i, 0]
        re = jnp.zeros(grad_ref.shape[3:], F32)
        im = re
        for o in range(channels):
            wr, wi = weight_ref[0, i, o], weight_ref[1, i, o]
            gr, gi = grads[o]
            re = re + (gr * wr + gi * wi)
            im = im + (gi * wr - gr * wi)
            outer_ref[0, i, o] = sr * gr + si * gi
            outer_ref[1, i, o] = sr * gi - si * gr
        out_ref[0, i, 0] = re
        out_ref[1, i, 0] = im
        return carry

    lax.fori_loop(0, weight_ref.shape[1], one, 0)


def params(collective_id=None):
    if collective_id is None:
        return pltpu.CompilerParams(vmem_limit_bytes=GRANT)
    return pltpu.CompilerParams(
        vmem_limit_bytes=GRANT, collective_id=collective_id, has_side_effects=True
    )


def whole(array):
    return pl.BlockSpec(array.shape, lambda *_: (0,) * array.ndim)


def planes_spec(shape):
    return pl.BlockSpec((1, shape[1], 1, shape[3], shape[4]), lambda x: (0, 0, x, 0, 0))


def shape_of(dims):
    return jax.ShapeDtypeStruct(dims, F32)


def local(plane_count, groups, field, cotangent, spec_weight, point_weight, bias):
    _, channels, local_planes, gy, gz = field.shape
    gx = local_planes * plane_count * groups
    kl = spec_weight.shape[3]
    modes = kl * plane_count // 2
    fl = spec_weight.shape[4] // modes
    width = channels // groups
    lanes = 2 * width * modes
    tile = min(128, fl * modes)
    per, tiles = tile // modes, fl * modes // tile
    order = np.arange(2 * modes).reshape(groups, tiles, per).transpose(2, 0, 1).reshape(-1)
    tables = Tables(gx, gy, gz, modes, width, order)
    y, z, x = jnp.asarray(tables.y), jnp.asarray(tables.z), jnp.asarray(tables.x)
    y_inv, z_inv, x_inv = (
        jnp.asarray(tables.y_inv),
        jnp.asarray(tables.z_inv),
        jnp.asarray(tables.x_inv),
    )
    weighting = np.where(np.arange(tile) % modes == 0, 1.0, 2.0) / float(gx * gy * gz)
    scale = jnp.asarray(weighting.astype(np.float32)[None, :])
    mode_shape = (2, channels, tiles, kl, tile)
    plane_rows = pltpu.VMEM((gx, kl, lanes), F32)
    mode_rows = pltpu.VMEM((2, width, groups * tiles, kl, tile), F32)
    semaphores = pltpu.SemaphoreType.DMA((5 + kl,))
    plane_semaphores = pltpu.SemaphoreType.DMA((local_planes,))
    anywhere = pl.BlockSpec(memory_space=pl.ANY)
    smem = pl.BlockSpec(memory_space=pltpu.SMEM)
    plane_block = planes_spec(field.shape)

    spectrum = pl.pallas_call(
        functools.partial(first_kernel, plane_count, groups),
        grid=(local_planes,),
        in_specs=[plane_block, whole(y), whole(z), whole(x)],
        out_specs=anywhere,
        out_shape=shape_of(mode_shape),
        scratch_shapes=[plane_rows, plane_rows, mode_rows, semaphores],
        compiler_params=params(1),
        name="first",
    )(field, y, z, x)
    rows = 8 if kl % 8 == 0 else kl
    mode_grid = (tiles, kl // rows)
    mode_block = pl.BlockSpec((2, channels, 1, rows, tile), lambda n, k: (0, 0, n, k, 0))
    weight_block = pl.BlockSpec((2, channels, channels, rows, tile), lambda n, k: (0, 0, 0, k, n))
    scale_block = whole(scale)
    mixed = pl.pallas_call(
        mix_kernel,
        grid=mode_grid,
        in_specs=[mode_block, weight_block, scale_block],
        out_specs=mode_block,
        out_shape=shape_of(mode_shape),
        compiler_params=params(),
        name="mix",
    )(spectrum, spec_weight, scale)
    output, local_grad, grad_modes = pl.pallas_call(
        functools.partial(middle_kernel, plane_count, groups),
        grid=(local_planes,),
        in_specs=[smem, smem, anywhere, plane_block, plane_block]
        + [whole(y_inv), whole(z_inv), whole(x_inv), whole(y), whole(z), whole(x)],
        out_specs=[plane_block, plane_block, anywhere],
        out_shape=[shape_of(field.shape), shape_of(field.shape), shape_of(mode_shape)],
        scratch_shapes=[pltpu.VMEM((gy, channels * gz), F32)] * 2
        + [mode_rows, plane_rows, plane_rows, semaphores, plane_semaphores]
        + [plane_rows, plane_rows, mode_rows, semaphores],
        compiler_params=params(2),
        name="middle",
    )(
        point_weight,
        bias,
        mixed,
        field,
        cotangent,
        y_inv,
        z_inv,
        x_inv,
        y,
        z,
        x,
    )
    steps = tiles * (kl // rows)
    flat = output.reshape(-1, gz)
    flat_block = pl.BlockSpec(
        (flat.shape[0] // steps, gz), lambda n, k: (n * (kl // rows) + k, 0)
    )
    spectrum_grad, weight_grad, flat = pl.pallas_call(
        back_kernel,
        grid=mode_grid,
        in_specs=[mode_block, mode_block, weight_block, scale_block, flat_block],
        out_specs=[mode_block, weight_block, flat_block],
        out_shape=[shape_of(mode_shape), shape_of(spec_weight.shape), shape_of(flat.shape)],
        compiler_params=params(),
        name="back",
    )(spectrum, grad_modes, spec_weight, scale, flat)
    output = flat.reshape(output.shape)
    field_grad = pl.pallas_call(
        functools.partial(last_kernel, plane_count, groups),
        grid=(local_planes,),
        in_specs=[anywhere, plane_block, whole(y_inv), whole(z_inv), whole(x_inv)],
        out_specs=plane_block,
        out_shape=shape_of(field.shape),
        scratch_shapes=[mode_rows, plane_rows, plane_rows, semaphores, plane_semaphores],
        compiler_params=params(3),
        name="last",
    )(spectrum_grad, local_grad, y_inv, z_inv, x_inv)
    return (output, field_grad, weight_grad)


def solution(mesh):
    shard = P("groups", None, ("planes", "chan"), None, None)
    in_specs = (shard, shard, P(None, None, None, "planes", "chan"), P(), P())
    out_specs = (shard, shard, P("groups", None, None, "planes", "chan"))
    function = functools.partial(local, mesh.shape["planes"], mesh.shape["chan"])
    return jax.shard_map(
        function, mesh=mesh, in_specs=in_specs, out_specs=out_specs, check_vma=False
    )
```
